1024 devices in a mesh: row: 64 (over y, z_lo, core), slab: 16 (over x, z_hi).
Axes of the slice: x: 4, y: 4, z: 32 (z_hi: 4, z_lo: 8; z = z_hi * 8 + z_lo), core: 2. Of those that a mesh axis runs over, the one named last changes fastest.
Arguments:
- features: bfloat16 [256, 262144], P('slab', 'row'), may hold values from -6 to 6
- self_weight: bfloat16 [256, 256], replicated, may hold values from -0.375 to 0.375
- neigh_weight: bfloat16 [256, 256], replicated, may hold values from -0.375 to 0.375
- cotangent: bfloat16 [256, 262144], P(None, ('row', 'slab')), may hold values from -6 to 6
- degree: int32 [262144], P('row'), may hold values from 1 to 1040, as said below
- tile_count: int32 [2048], P('row'), may hold values from 1 to 8, as said below
- tile_cols: int32 [2048, 8], P('row'), may hold values from 0 to 2047
- tile_vals: bfloat16 [2048, 8, 128, 128], P('row'), may hold values from 0 to 1.5, as said below
Outputs:
- output: bfloat16 [256, 262144], P(None, ('row', 'slab'))
- grad_self: float32 [256, 256], P('slab')
- grad_neigh: float32 [256, 256], P('slab')
The draws below stay inside these ranges and needn't reach their ends.
Inputs may be any that keep to these rules, and one draw needn't show every extreme that they name: `tile_count`: every row of tiles uses between 1 and 8 slots; in every eight consecutive row blocks of 4096 nodes one (drawn) has all 8 slots used in each of its rows of tiles, the others use at most half of the slots. `tile_vals`: nonnegative edge weights, most of them zero. A node's degree is at least one more than the number of nonzero weights in its row of its used tile slots.
All inputs are finite; a program needn't handle non-finite values.
Results may differ from the reference program's by a relative error of at most 0.0029.
Values may be sent and summed in bfloat16 or wider, within the bound.
A program may use at most 64 MiB of HBM per device.

```python
import math
import jax
import jax.numpy as jnp
from jax import lax

D = 256
TILE = 128
KT = 8
ROWS_DEV = 4096
NODES = 262144
NT = 2048


def slot_counts(key):
    count_key = jax.random.fold_in(key, 11)
    light_key, heavy_key = jax.random.split(count_key)
    light_count = jax.random.randint(light_key, (NT,), 1, max(KT // 2, 1) + 1, dtype=jnp.int32)
    offset = jax.random.randint(heavy_key, (), 0, 8, dtype=jnp.int32)
    owner_block = jnp.arange(NT, dtype=jnp.int32) // (ROWS_DEV // TILE)
    heavy_rows = (owner_block + offset) % 8 == 0
    return jnp.where(heavy_rows, KT, light_count).astype(jnp.int32)


def edge_mask(key):
    mask_key = jax.random.fold_in(key, 17)
    return jax.random.randint(mask_key, (NT, KT, TILE, TILE), 0, 64, dtype=jnp.int32) == 0


def draw_tile_count(key, part):
    return slot_counts(key)


def draw_tile_vals(key, part):
    present = edge_mask(key)
    key = jax.random.fold_in(key, 23)
    lowest = 0.5
    weights = jax.random.uniform(key, (NT, KT, TILE, TILE), dtype=jnp.float32, minval=lowest, maxval=1.5)
    return jnp.where(present, weights, jnp.float32(0.0)).astype(jnp.bfloat16)


def draw_degree(key, part):
    present = edge_mask(key).astype(jnp.int32)
    counts = slot_counts(key)
    key = jax.random.fold_in(key, 37)
    remainder_key, pick_key = jax.random.split(key)
    active = (jnp.arange(KT, dtype=jnp.int32)[None, :] < counts[:, None]).astype(jnp.int32)
    per_slot = jnp.sum(present, axis=3)
    in_panel = jnp.sum(per_slot * active[:, :, None], axis=1).reshape(NODES)
    remainder = jax.random.randint(remainder_key, (NODES,), 1, 17, dtype=jnp.int32)
    chosen = jax.random.randint(pick_key, (), 0, NODES, dtype=jnp.int32)
    largest = jnp.int32(KT * TILE + 16)
    drawn = in_panel + remainder
    return jnp.where(jnp.arange(NODES, dtype=jnp.int32) == chosen, largest, drawn).astype(jnp.int32)


def plant(array, stream_key, low, top_value):
    extent = array.shape
    spot = [jax.random.randint(jax.random.fold_in(stream_key, axis), (), 0, extent[axis]) for axis in range(len(extent))]
    array = array.at[tuple(spot)].set(low)
    longest = extent.index(max(extent))
    spot[longest] = (spot[longest] + 1) % extent[longest]
    return array.at[tuple(spot)].set(top_value)


def levels(stream_key, extent, cuts, least, high):
    level = 1.0
    for axis_at, shards_of in cuts:
        steps = jax.random.uniform(jax.random.fold_in(jax.random.fold_in(stream_key, 6), axis_at), (shards_of,), jnp.float32, least / len(cuts), high / len(cuts))
        level = level * jnp.repeat(jnp.exp(steps), extent[axis_at] // shards_of).reshape((-1,) + (1,) * (len(extent) - 1 - axis_at))
    return level


def scatter_about(rng, extent, deviation, most, cuts=(), kind=jnp.bfloat16):
    factor_of = levels(rng, extent, cuts, -0.22, 0.18) if cuts else 1.0
    entries = jax.random.normal(rng, extent, jnp.float32) * deviation * factor_of
    return jnp.minimum(jnp.maximum(entries, -most), most).astype(kind)


def setup_inputs(seed: int = 0) -> dict:
    key_of = jax.random.split(jax.random.key(seed), 9)
    return {
        "features": scatter_about(key_of[0], (D, NODES), 1.0, 6.0, ((0, 16), (1, 64))),
        "self_weight": scatter_about(key_of[1], (D, D), D ** -0.5, 0.375),
        "neigh_weight": scatter_about(key_of[2], (D, D), D ** -0.5, 0.375),
        "cotangent": scatter_about(key_of[3], (D, NODES), 1.0, 6.0, ((1, 1024),)),
        "degree": draw_degree(jax.random.fold_in(key_of[8], 71), 0),
        "tile_count": draw_tile_count(jax.random.fold_in(key_of[8], 71), 0),
        "tile_cols": plant(jax.random.randint(key_of[6], (NT, KT), 0, NT), jax.random.fold_in(key_of[6], 1), 0, NT - 1).astype(jnp.int32),
        "tile_vals": draw_tile_vals(jax.random.fold_in(key_of[8], 71), 0),
    }


def reference(features, self_weight, neigh_weight, cotangent, degree, tile_count, tile_cols, tile_vals):
    blocks = features.reshape(D, NT, TILE)

    def row_tile(items):
        column_ids, count_here, weights = items
        picked = jnp.take(blocks, column_ids, axis=1).astype(jnp.float32)
        active = jnp.arange(KT, dtype=jnp.int32) < count_here
        masked = jnp.where(active[:, None, None], weights.astype(jnp.float32), jnp.float32(0.0))
        return jnp.einsum('fkc,kdc->fd', picked, masked)
    sums = lax.map(row_tile, (tile_cols, tile_count, tile_vals))
    summed = jnp.transpose(sums, (1, 0, 2)).reshape(D, NODES)
    mean_agg = (summed / degree.astype(jnp.float32)[None, :]).astype(jnp.bfloat16)
    feat_wide = features.astype(jnp.float32)
    mean_wide = mean_agg.astype(jnp.float32)
    projected = jnp.einsum('io,in->on', self_weight.astype(jnp.float32), feat_wide)
    projected = projected + jnp.einsum('io,in->on', neigh_weight.astype(jnp.float32), mean_wide)
    output = projected.astype(jnp.bfloat16)
    factor = 1.0 / math.sqrt(NODES)
    cot_wide = cotangent.astype(jnp.float32)
    grad_self = jnp.einsum('in,on->io', feat_wide, cot_wide) * factor
    grad_neigh = jnp.einsum('in,on->io', mean_wide, cot_wide) * factor
    return (output, grad_self, grad_neigh)
```

```python
import functools
import math

import jax
import jax.numpy as jnp
from jax import lax
from jax.experimental import pallas as pl
from jax.experimental.pallas import tpu as pltpu
from jax.sharding import PartitionSpec as P

NY, NZ, NC = 4, 8, 2
NX, NH = 4, 4
NROW, NSLAB = NY * NZ * NC, NX * NH
WIDTH = 256
TILE = 128
MESH = pl.DeviceIdType.MESH


def nt_dot(a, b):
    return lax.dot_general(a, b, (((1,), (1,)), ((), ())), preferred_element_type=jnp.float32)


def tn_dot(a, b):
    return lax.dot_general(a, b, (((0,), (0,)), ((), ())), preferred_element_type=jnp.float32)


def kernel(
    factor,
    cols_ref,
    feat_ref,
    deg_ref,
    self_ref,
    neigh_ref,
    cot_hbm,
    vals_hbm,
    out_ref,
    gself_ref,
    gneigh_ref,
    buf,
    vals,
    cot,
    mean,
    fown,
    mown,
    oself,
    g,
    r1,
    acc,
    r2,
    acc2,
    r3,
    acc3,
    r4,
    r5,
    r6,
    local_sem,
    zsend,
    ysend,
    hsend,
    csend,
    recv,
    hrecv,
    crecv,
    fsend,
    frecv,
    msend,
    mrecv,
    send1,
    recv1,
    send2,
    recv2,
    send3,
    recv3,
    send4,
    recv4,
    send5,
    recv5,
    send6,
    recv6,
):
    row = lax.axis_index("row")
    slab = lax.axis_index("slab")
    core = lax.rem(row, NC)
    z = lax.rem(lax.div(row, NC), NZ)
    y = lax.div(row, NC * NZ)
    x = lax.div(slab, NH)
    hi = lax.rem(slab, NH)
    per_block = feat_ref.shape[1] // TILE
    half = per_block // 2

    def row_of(yy, zz, cc):
        return (yy * NZ + zz) * NC + cc

    vals_copy = pltpu.make_async_copy(vals_hbm, vals, local_sem.at[0])
    vals_copy.start()
    cot_copy = pltpu.make_async_copy(cot_hbm, cot, local_sem.at[1])
    cot_copy.start()
    for j in range(per_block):
        buf[row * per_block + j] = feat_ref[:, j * TILE : (j + 1) * TILE]
    buf[NROW * per_block] = jnp.zeros((feat_ref.shape[0], TILE), jnp.bfloat16)

    barrier = pltpu.get_barrier_semaphore()
    partners = 0
    for d in range(1, NSLAB):
        pl.semaphore_signal(
            barrier, inc=1, device_id=(row, lax.rem(slab + d, NSLAB)), device_id_type=MESH
        )
        partners += 1
    for d in range(1, NZ):
        pl.semaphore_signal(
            barrier, inc=1, device_id=(row_of(y, lax.rem(z + d, NZ), core), slab), device_id_type=MESH
        )
        partners += 1
    for d in range(NY):
        for e in range(NC):
            if d or e:
                pl.semaphore_signal(
                    barrier,
                    inc=1,
                    device_id=(row_of(lax.rem(y + d, NY), z, lax.rem(core + e, NC)), slab),
                    device_id_type=MESH,
                )
                partners += 1
    pl.semaphore_wait(barrier, partners)

    yup, ydown, yopp = lax.rem(y + 1, NY), lax.rem(y + 3, NY), lax.rem(y + 2, NY)
    mate = row_of(y, z, 1 - core)

    def block(yy, zz, cc):
        return buf.at[pl.ds(row_of(yy, zz, cc) * per_block, per_block)]

    def half_block(yy, zz, which):
        return buf.at[pl.ds(row_of(yy, zz, core) * per_block + which * half, half)]

    def block_copy(yy, zz, send, arrive, target):
        ref = block(yy, zz, core)
        return pltpu.make_async_remote_copy(
            src_ref=ref,
            dst_ref=ref,
            send_sem=send,
            recv_sem=arrive,
            device_id=(target, slab),
            device_id_type=MESH,
        )

    def z_copy(way, zz):
        target = row_of(y, z + (1 - 2 * way), core)
        return block_copy(y, zz, zsend.at[way, zz], recv.at[y, zz], target)

    def y_copy(way, zz):
        target = row_of(ydown if way else yup, z, core)
        return block_copy(y, zz, ysend.at[way, zz], recv.at[y, zz], target)

    def h_copy(way, zz):
        source = yup if way else ydown
        target = row_of(ydown if way else yup, z, core)
        ref = half_block(source, zz, way)
        return pltpu.make_async_remote_copy(
            src_ref=ref,
            dst_ref=ref,
            send_sem=hsend.at[way, zz],
            recv_sem=hrecv.at[way, zz],
            device_id=(target, slab),
            device_id_type=MESH,
        )

    def c_copy(yy, zz):
        return block_copy(yy, zz, csend.at[yy, zz], crecv.at[yy, zz], mate)

    def arrived(yy, zz):
        block_copy(yy, zz, csend.at[yy, zz], recv.at[yy, zz], mate).wait_recv()

    def spread(zz):
        y_copy(0, zz).start()
        y_copy(1, zz).start()
        c_copy(y, zz).start()

    def relay(zz):
        arrived(ydown, zz)
        h_copy(0, zz).start()
        c_copy(ydown, zz).start()
        arrived(yup, zz)
        h_copy(1, zz).start()
        c_copy(yup, zz).start()

    def finish(zz):
        for way in range(2):
            ref = half_block(yopp, zz, way)
            pltpu.make_async_remote_copy(
                src_ref=ref,
                dst_ref=ref,
                send_sem=hsend.at[way, zz],
                recv_sem=hrecv.at[way, zz],
                device_id=(mate, slab),
                device_id_type=MESH,
            ).wait_recv()
        c_copy(yopp, zz).start()

    def f_copy(other):
        return pltpu.make_async_remote_copy(
            src_ref=feat_ref.at[:, pl.ds(pl.multiple_of(other * WIDTH, WIDTH), WIDTH)],
            dst_ref=fown.at[pl.ds(pl.multiple_of(slab * 16, 16), 16), :],
            send_sem=fsend.at[other],
            recv_sem=frecv.at[slab],
            device_id=(row, other),
            device_id_type=MESH,
        )

    def f_wait(other):
        pltpu.make_async_remote_copy(
            src_ref=feat_ref.at[:, pl.ds(0, WIDTH)],
            dst_ref=fown.at[pl.ds(pl.multiple_of(other * 16, 16), 16), :],
            send_sem=fsend.at[other],
            recv_sem=frecv.at[other],
            device_id=(row, other),
            device_id_type=MESH,
        ).wait_recv()

    @pl.when(z < NZ - 1)
    def _():
        z_copy(0, z).start()

    @pl.when(z > 0)
    def _():
        z_copy(1, z).start()

    spread(z)
    LAG, LAG2 = 1, 2

    @pl.loop(1, NZ + LAG2)
    def _(t):
        @pl.when((t < NZ) & (z - t >= 0))
        def _():
            zz = z - t
            arrived(y, zz)

            @pl.when(z < NZ - 1)
            def _():
                z_copy(0, zz).start()

            spread(zz)

        @pl.when((t < NZ) & (z + t < NZ))
        def _():
            zz = z + t
            arrived(y, zz)

            @pl.when(z > 0)
            def _():
                z_copy(1, zz).start()

            spread(zz)

        @pl.when(t == 3)
        def _():
            @pl.loop(1, NSLAB)
            def _(d):
                f_copy(lax.rem(slab + d, NSLAB)).start()

        u = t - LAG

        @pl.when((u < NZ) & (z - u >= 0))
        def _():
            relay(z - u)

        @pl.when((u > 0) & (u < NZ) & (z + u < NZ))
        def _():
            relay(z + u)

        v = t - LAG2

        @pl.when((v >= 0) & (v < NZ) & (z - v >= 0))
        def _():
            finish(z - v)

        @pl.when((v > 0) & (v < NZ) & (z + v < NZ))
        def _():
            finish(z + v)

    @pl.loop(1, NSLAB)
    def _(d):
        f_wait(lax.rem(slab + d, NSLAB))

    fown[pl.ds(pl.multiple_of(slab * 16, 16), 16), :] = feat_ref[
        :, pl.ds(pl.multiple_of(slab * WIDTH, WIDTH), WIDTH)
    ]
    cot_copy.wait()
    oself[...] = tn_dot(self_ref[...], fown[...])

    def keep_grad(q, values):
        for h in range(NC):
            for xx in range(NX):
                for hh in range(NH):
                    for e in range(2):
                        at = (xx * NH + hh) * 16 + e * 8
                        g[h, xx, 2 * q + e, hh] = values[at : at + 8, h * TILE : (h + 1) * TILE]

    keep_grad(0, nt_dot(fown[...], cot[...]))

    vals_copy.wait()

    @pl.loop(0, NY)
    def _(yy):
        @pl.loop(0, NZ)
        def _(zz):
            ref = block(yy, zz, 1 - core)
            pltpu.make_async_remote_copy(
                src_ref=ref,
                dst_ref=ref,
                send_sem=csend.at[yy, zz],
                recv_sem=crecv.at[yy, zz],
                device_id=(mate, slab),
                device_id_type=MESH,
            ).wait_recv()

    def m_copy(other):
        return pltpu.make_async_remote_copy(
            src_ref=mean.at[other],
            dst_ref=mown.at[pl.ds(pl.multiple_of(slab * 16, 16), 16), :],
            send_sem=msend.at[other],
            recv_sem=mrecv.at[slab],
            device_id=(row, other),
            device_id_type=MESH,
        )

    def m_wait(other):
        pltpu.make_async_remote_copy(
            src_ref=mean.at[other],
            dst_ref=mown.at[pl.ds(pl.multiple_of(other * 16, 16), 16), :],
            send_sem=msend.at[other],
            recv_sem=mrecv.at[other],
            device_id=(row, other),
            device_id_type=MESH,
        ).wait_recv()

    slots = cols_ref.shape[1]

    @pl.loop(0, NSLAB)
    def _(d):
        other = lax.rem(slab + 1 + d, NSLAB)
        for p in range(2):
            t = other * 2 + p
            picked = [buf[cols_ref[t, k]] for k in range(slots)]
            weights = jnp.concatenate([vals[t, k] for k in range(slots)], axis=1)
            total = nt_dot(jnp.concatenate(picked, axis=1), weights)
            degree = deg_ref[pl.ds(t, 1), :].astype(jnp.float32)
            mean[other, :, p * TILE : (p + 1) * TILE] = (total / degree).astype(jnp.bfloat16)

        @pl.when(d < NSLAB - 1)
        def _():
            m_copy(other).start()

    mown[pl.ds(pl.multiple_of(slab * 16, 16), 16), :] = mean[slab]

    @pl.loop(1, NSLAB)
    def _(d):
        m_wait(lax.rem(slab + d, NSLAB))

    keep_grad(1, nt_dot(mown[...], cot[...]))

    copy1 = pltpu.make_async_remote_copy(
        src_ref=g.at[1 - core],
        dst_ref=r1,
        send_sem=send1,
        recv_sem=recv1,
        device_id=(mate, slab),
        device_id_type=MESH,
    )
    copy1.start()
    out_ref[...] = (oself[...] + tn_dot(neigh_ref[...], mown[...])).astype(jnp.bfloat16)
    copy1.wait_recv()
    acc[...] = g[core] + r1[...]

    def stage(src, dst, sends, recvs, size, me, target):
        copies = []
        for d in range(1, size):
            other = lax.rem(me + d, size)
            copies.append(
                pltpu.make_async_remote_copy(
                    src_ref=src(other),
                    dst_ref=dst.at[me],
                    send_sem=sends.at[other],
                    recv_sem=recvs.at[me],
                    device_id=target(other),
                    device_id_type=MESH,
                )
            )
        for c in copies:
            c.start()
        return copies

    def take(src, dst, sends, recvs, size, me, target):
        for d in range(1, size):
            other = lax.rem(me + d, size)
            pltpu.make_async_remote_copy(
                src_ref=src(other),
                dst_ref=dst.at[other],
                send_sem=sends.at[other],
                recv_sem=recvs.at[other],
                device_id=target(other),
                device_id_type=MESH,
            ).wait_recv()

    def exchange(*a):
        copies = stage(*a)
        take(*a)
        return copies

    started = []
    started += exchange(
        lambda o: acc.at[o], r2, send2, recv2, NX, x, lambda o: (row, o * NH + hi)
    )
    total = acc[x]
    for d in range(1, NX):
        total = total + r2[lax.rem(x + d, NX)]
    acc2[...] = total
    started += exchange(
        lambda o: acc2.at[o], r3, send3, recv3, NY, y, lambda o: (row_of(o, z, core), slab)
    )
    total = acc2[y]
    for d in range(1, NY):
        total = total + r3[lax.rem(y + d, NY)]
    acc3[...] = total
    started += exchange(
        lambda o: acc3.at[o], r4, send4, recv4, NH, hi, lambda o: (row, x * NH + o)
    )
    total = acc3[hi]
    for d in range(1, NH):
        total = total + r4[lax.rem(hi + d, NH)]
    r5[z] = total
    started += exchange(
        lambda o: r5.at[z], r5, send5, recv5, NZ, z, lambda o: (row_of(y, o, core), slab)
    )
    total = r5[0]
    for i in range(1, NZ):
        total = total + r5[i]
    spot = y * NC + core
    r6[spot] = total * factor
    started += exchange(
        lambda o: r6.at[spot],
        r6,
        send6,
        recv6,
        NY * NC,
        spot,
        lambda o: (row_of(lax.div(o, NC), z, lax.rem(o, NC)), slab),
    )
    for q, ref in enumerate((gself_ref, gneigh_ref)):
        for e in range(2):
            for c in range(NC):
                ref[e * 8 : (e + 1) * 8, c * TILE : (c + 1) * TILE] = r6[(2 * q + e) * NC + c]

    for c in started:
        c.wait_send()
    copy1.wait_send()

    @pl.loop(1, NSLAB)
    def _(d):
        f_copy(lax.rem(slab + d, NSLAB)).wait_send()
        m_copy(lax.rem(slab + d, NSLAB)).wait_send()

    @pl.loop(0, NZ)
    def _(zz):
        @pl.when((z < NZ - 1) & (zz <= z))
        def _():
            z_copy(0, zz).wait_send()

        @pl.when((z > 0) & (zz >= z))
        def _():
            z_copy(1, zz).wait_send()

        for way in range(2):
            y_copy(way, zz).wait_send()
            h_copy(way, zz).wait_send()

        @pl.loop(0, NY)
        def _(yy):
            c_copy(yy, zz).wait_send()


def per_device(
    features, self_weight, neigh_weight, cotangent, degree, tile_count, tile_cols, tile_vals
):
    width, nodes = features.shape
    tiles, slots = tile_cols.shape
    factor = 1.0 / math.sqrt(nodes * NROW)
    f32, bf16 = jnp.float32, jnp.bfloat16
    dma = pltpu.SemaphoreType.DMA
    vmem = pl.BlockSpec(memory_space=pltpu.VMEM)
    smem = pl.BlockSpec(memory_space=pltpu.SMEM)
    hbm = pl.BlockSpec(memory_space=pl.ANY)
    return pl.pallas_call(
        functools.partial(kernel, factor),
        out_shape=(
            jax.ShapeDtypeStruct((WIDTH, WIDTH), bf16),
            jax.ShapeDtypeStruct((width, WIDTH), f32),
            jax.ShapeDtypeStruct((width, WIDTH), f32),
        ),
        in_specs=[smem, vmem, vmem, vmem, vmem, hbm, hbm],
        out_specs=(vmem, vmem, vmem),
        scratch_shapes=[
            pltpu.VMEM((NROW * tiles + 1, width, TILE), bf16),
            pltpu.VMEM(tile_vals.shape, bf16),
            pltpu.VMEM((WIDTH, WIDTH), bf16),
            pltpu.VMEM((NSLAB, width, WIDTH), bf16),
            pltpu.VMEM((WIDTH, WIDTH), bf16),
            pltpu.VMEM((WIDTH, WIDTH), bf16),
            pltpu.VMEM((WIDTH, WIDTH), f32),
            pltpu.VMEM((NC, NX, NY, NH, 8, TILE), f32),
            pltpu.VMEM((NX, NY, NH, 8, TILE), f32),
            pltpu.VMEM((NX, NY, NH, 8, TILE), f32),
            pltpu.VMEM((NX, NY, NH, 8, TILE), f32),
            pltpu.VMEM((NY, NH, 8, TILE), f32),
            pltpu.VMEM((NY, NH, 8, TILE), f32),
            pltpu.VMEM((NH, 8, TILE), f32),
            pltpu.VMEM((NH, 8, TILE), f32),
            pltpu.VMEM((NZ, 8, TILE), f32),
            pltpu.VMEM((NY * NC, 8, TILE), f32),
            dma((2,)),
            dma((2, NZ)),
            dma((2, NZ)),
            dma((2, NZ)),
            dma((NY, NZ)),
            dma((NY, NZ)),
            dma((2, NZ)),
            dma((NY, NZ)),
            dma((NSLAB,)),
            dma((NSLAB,)),
            dma((NSLAB,)),
            dma((NSLAB,)),
            dma(()),
            dma(()),
            dma((NX,)),
            dma((NX,)),
            dma((NY,)),
            dma((NY,)),
            dma((NH,)),
            dma((NH,)),
            dma((NZ,)),
            dma((NZ,)),
            dma((NY * NC,)),
            dma((NY * NC,)),
        ],
        compiler_params=pltpu.CompilerParams(
            collective_id=0, has_side_effects=True, vmem_limit_bytes=40 * 1024 * 1024
        ),
    )(
        jnp.where(jnp.arange(slots)[None, :] < tile_count[:, None], tile_cols, NROW * tiles),
        features,
        degree.reshape(tiles, TILE),
        self_weight,
        neigh_weight,
        cotangent,
        tile_vals,
    )


def solution(mesh):
    return jax.shard_map(
        per_device,
        mesh=mesh,
        in_specs=(
            P("slab", "row"),
            P(),
            P(),
            P(None, ("row", "slab")),
            P("row"),
            P("row"),
            P("row", None),
            P("row", None, None, None),
        ),
        out_specs=(P(None, ("row", "slab")), P("slab", None), P("slab", None)),
        check_vma=False,
    )
```

```python
import functools
import math

import jax
import jax.numpy as jnp
from jax import lax
from jax.experimental import pallas as pl
from jax.experimental.pallas import tpu as pltpu
from jax.sharding import PartitionSpec as P

NY, NZ, NC = 4, 8, 2
NX, NH = 4, 4
NROW, NSLAB = NY * NZ * NC, NX * NH
WIDTH = 256
TILE = 128
PART = 16
ROUNDS = (1, 2, 4, 8, 1)
MESH = pl.DeviceIdType.MESH


def nt_dot(a, b):
    return lax.dot_general(a, b, (((1,), (1,)), ((), ())), preferred_element_type=jnp.float32)


def tn_dot(a, b):
    return lax.dot_general(a, b, (((0,), (0,)), ((), ())), preferred_element_type=jnp.float32)


def wrap(value, size):
    return jnp.where(value >= size, value - size, value)


def kernel(
    factor,
    index_ref,
    feat_hbm,
    vals_hbm,
    cot_hbm,
    self_hbm,
    neigh_hbm,
    deg_hbm,
    out_ref,
    gself_ref,
    gneigh_ref,
    feat,
    vals,
    self_ref,
    neigh_ref,
    deg_ref,
    buf,
    cot,
    fown,
    mean,
    mown,
    oself,
    g,
    ra,
    acc,
    rb,
    acc2,
    rh,
    rz,
    rd,
    told,
    local_sem,
    zsend,
    ysend,
    hsend,
    csend,
    recv,
    hrecv,
    crecv,
    fsend,
    frecv,
    msend,
    mrecv,
    asend,
    arecv,
    bsend,
    brecv,
    hisend,
    hirecv,
    zlsend,
    zlrecv,
    dsend,
    drecv,
):
    row = lax.axis_index("row")
    slab = lax.axis_index("slab")
    core = lax.rem(row, NC)
    z = lax.rem(lax.div(row, NC), NZ)
    y = lax.div(row, NC * NZ)
    x = lax.div(slab, NH)
    hi = lax.rem(slab, NH)
    mate = row + 1 - 2 * core
    per_block = feat.shape[1] // TILE
    half = per_block // 2

    def row_of(yy, zz, cc):
        return (yy * NZ + zz) * NC + cc

    def start_of(yy, zz, cc):
        return ((cc * NY + yy) * NZ + zz) * per_block

    def remote(src, dst, send, arrive, device):
        return pltpu.make_async_remote_copy(
            src_ref=src,
            dst_ref=dst,
            send_sem=send,
            recv_sem=arrive,
            device_id=device,
            device_id_type=MESH,
        )

    barrier = pltpu.get_barrier_semaphore()
    def along(d):
        at = lax.rem(hi * NZ + z + d + NH * NZ, NH * NZ)
        return (row_of(y, lax.rem(at, NZ), core), x * NH + lax.div(at, NZ))

    partners = [along(1), along(-1), (mate, slab)]
    partners += [
        (r, wrap(x + d, NX) * NH + hi) for d in range(1, NX) for r in (row, mate)
    ]
    partners += [
        (row_of(wrap(y + d, NY), z, c), slab) for d in range(1, NY) for c in range(NC)
    ]
    for partner in partners:
        pl.semaphore_signal(barrier, inc=1, device_id=partner, device_id_type=MESH)
    loads = [
        pltpu.make_async_copy(src, dst, local_sem.at[i])
        for i, (src, dst) in enumerate(
            (
                (feat_hbm, feat),
                (cot_hbm, cot),
                (vals_hbm, vals),
                (self_hbm, self_ref),
                (neigh_hbm, neigh_ref),
                (deg_hbm, deg_ref),
            )
        )
    ]
    for load in loads:
        load.start()
    loads[0].wait()
    own = start_of(y, z, core)
    for j in range(per_block):
        buf[own + j] = feat[:, j * TILE : (j + 1) * TILE]
    buf[NROW * per_block] = jnp.zeros((PART, TILE), jnp.bfloat16)
    pl.semaphore_wait(barrier, len(partners))

    def tell(k):
        for side, step in enumerate((ROUNDS[k], -ROUNDS[k])):
            pl.semaphore_signal(
                told.at[k, side], inc=1, device_id=along(step), device_id_type=MESH
            )

    def hear(k):
        for side in range(2):
            pl.semaphore_wait(told.at[k, side], 1)

    tell(0)
    yup, ydown, yopp = wrap(y + 1, NY), wrap(y + 3, NY), wrap(y + 2, NY)

    def block(yy, zz, cc):
        return buf.at[pl.ds(start_of(yy, zz, cc), per_block)]

    def half_block(yy, zz, which):
        return buf.at[pl.ds(start_of(yy, zz, core) + which * half, half)]

    def z_copy(way, zz):
        ref = block(y, zz, core)
        target = row_of(y, z + 1 - 2 * way, core)
        return remote(ref, ref, zsend.at[way, zz], recv.at[y, zz], (target, slab))

    def z_out(way, zz):
        @pl.when((z > 0) if way else (z < NZ - 1))
        def _():
            z_copy(way, zz).start()

    def y_copy(way, zz):
        ref = block(y, zz, core)
        target = row_of(ydown if way else yup, z, core)
        return remote(ref, ref, ysend.at[way, zz], recv.at[y, zz], (target, slab))

    def h_copy(way, zz):
        ref = half_block(yup if way else ydown, zz, way)
        target = row_of(ydown if way else yup, z, core)
        return remote(ref, ref, hsend.at[way, zz], hrecv.at[way, zz], (target, slab))

    def c_copy(yy, zz):
        ref = block(yy, zz, core)
        return remote(ref, ref, csend.at[yy, zz], crecv.at[yy, zz], (mate, slab))

    def arrived(yy, zz):
        ref = block(yy, zz, core)
        remote(ref, ref, csend.at[yy, zz], recv.at[yy, zz], (mate, slab)).wait_recv()

    def spread(zz):
        y_copy(0, zz).start()
        y_copy(1, zz).start()
        c_copy(y, zz).start()

    def relay(zz):
        arrived(ydown, zz)
        h_copy(0, zz).start()
        c_copy(ydown, zz).start()
        arrived(yup, zz)
        h_copy(1, zz).start()
        c_copy(yup, zz).start()

    def finish(zz):
        for way in range(2):
            ref = half_block(yopp, zz, way)
            remote(ref, ref, hsend.at[way, zz], hrecv.at[way, zz], (mate, slab)).wait_recv()
        c_copy(yopp, zz).start()

    def f_copy(other):
        src = feat.at[:, pl.ds(pl.multiple_of(other * WIDTH, WIDTH), WIDTH)]
        dst = fown.at[pl.ds(pl.multiple_of(slab * PART, PART), PART), :]
        return remote(src, dst, fsend.at[other], frecv.at[slab], (row, other))

    z_out(0, z)
    z_out(1, z)
    spread(z)
    LAG, LAG2 = 1, 2

    @pl.loop(1, NZ + LAG2)
    def _(t):
        @pl.when((t < NZ) & (z - t >= 0))
        def _():
            arrived(y, z - t)
            z_out(0, z - t)
            spread(z - t)

        @pl.when((t < NZ) & (z + t < NZ))
        def _():
            arrived(y, z + t)
            z_out(1, z + t)
            spread(z + t)

        for k, when in enumerate((1, 2, 3, 4, 5)):

            @pl.when(t == when)
            def _():
                hear(k)
                if k + 1 < len(ROUNDS):
                    tell(k + 1)
                else:

                    @pl.loop(1, NSLAB)
                    def _(d):
                        f_copy(wrap(slab + d, NSLAB)).start()

        u = t - LAG

        @pl.when((u < NZ) & (z - u >= 0))
        def _():
            relay(z - u)

        @pl.when((u > 0) & (u < NZ) & (z + u < NZ))
        def _():
            relay(z + u)

        v = t - LAG2

        @pl.when((v >= 0) & (v < NZ) & (z - v >= 0))
        def _():
            finish(z - v)

        @pl.when((v > 0) & (v < NZ) & (z + v < NZ))
        def _():
            finish(z + v)

    a_peers = [
        (wrap(core + e, NC), wrap(x + d, NX)) for d in range(NX) for e in range(NC) if d or e
    ]
    y_peers = [wrap(y + d, NY) for d in range(1, NY)]
    h_peers = [wrap(hi + d, NH) for d in range(1, NH)]
    z_peers = [wrap(z + d, NZ) for d in range(1, NZ)]
    d_peers = [(yy, c) for yy in y_peers for c in range(NC)] + [(y, 1 - core)]

    def a_copy(q, peer, arriving=False):
        cc, xx = peer
        mine = (cc, xx) if arriving else (core, x)
        device = (row_of(y, z, cc), xx * NH + hi)
        return remote(
            g.at[q, cc, xx],
            ra.at[q, mine[0], mine[1]],
            asend.at[q, cc, xx],
            arecv.at[q, mine[0], mine[1]],
            device,
        )

    def b_copy(yy, arriving=False):
        mine = yy if arriving else y
        device = (row_of(yy, z, core), slab)
        return remote(acc.at[yy], rb.at[mine], bsend.at[yy], brecv.at[mine], device)

    def hi_copy(hh, arriving=False):
        mine = hh if arriving else hi
        device = (row, x * NH + hh)
        return remote(acc2.at[hh], rh.at[mine], hisend.at[hh], hirecv.at[mine], device)

    def zl_copy(zz, arriving=False):
        mine = zz if arriving else z
        device = (row_of(y, zz, core), slab)
        return remote(rz.at[z], rz.at[mine], zlsend.at[zz], zlrecv.at[mine], device)

    def d_copy(peer, arriving=False):
        yy, c = peer
        mine = (yy, c) if arriving else (y, core)
        device = (row_of(yy, z, c), slab)
        return remote(
            rd.at[y, core],
            rd.at[mine[0], mine[1]],
            dsend.at[yy, c],
            drecv.at[mine[0], mine[1]],
            device,
        )

    def begin_sum(q, left):
        total = nt_dot(left, cot[...])
        for c in range(NC):
            for xx in range(NX):
                for hh in range(NH):
                    for e in range(2):
                        at = (xx * NH + hh) * PART + e * 8
                        g[q, c, xx, e, hh] = total[at : at + 8, c * TILE : (c + 1) * TILE]
        for peer in a_peers:
            a_copy(q, peer).start()

    def after_a(q):
        total = g[q, core, x]
        for peer in a_peers:
            a_copy(q, peer, True).wait_recv()
            total = total + ra[q, peer[0], peer[1]]
        acc[2 * q : 2 * q + 2] = total

    @pl.loop(0, NY)
    def _(yy):
        @pl.loop(0, NZ)
        def _(zz):
            ref = block(yy, zz, 1 - core)
            remote(
                ref, ref, csend.at[yy, zz], crecv.at[yy, zz], (mate, slab)
            ).wait_recv()

    loads[2].wait()
    loads[5].wait()

    def m_copy(other):
        dst = mown.at[pl.ds(pl.multiple_of(slab * PART, PART), PART), :]
        return remote(mean.at[other], dst, msend.at[other], mrecv.at[slab], (row, other))

    slots = index_ref.shape[0]

    @pl.loop(0, NH)
    def _(dh):
        hh = wrap(wrap(hi + 2, NH) + dh, NH)

        @pl.loop(0, NX)
        def _(dx):
            other = wrap(x + 1 + dx, NX) * NH + hh
            for p in range(2):
                t = other * 2 + p
                picked = [buf[index_ref[k, t]] for k in range(slots)]
                weights = jnp.concatenate([vals[t, k] for k in range(slots)], axis=1)
                total = nt_dot(jnp.concatenate(picked, axis=1), weights)
                degree = deg_ref[pl.ds(t, 1), :].astype(jnp.float32)
                mean[other, :, p * TILE : (p + 1) * TILE] = (total / degree).astype(jnp.bfloat16)

            @pl.when(other != slab)
            def _():
                m_copy(other).start()

    mown[pl.ds(pl.multiple_of(slab * PART, PART), PART), :] = mean[slab]

    fown[pl.ds(pl.multiple_of(slab * PART, PART), PART), :] = feat[
        :, pl.ds(pl.multiple_of(slab * WIDTH, WIDTH), WIDTH)
    ]
    loads[1].wait()

    @pl.loop(1, NSLAB)
    def _(d):
        other = wrap(slab + d, NSLAB)
        dst = fown.at[pl.ds(pl.multiple_of(other * PART, PART), PART), :]
        src = feat.at[:, pl.ds(0, WIDTH)]
        remote(src, dst, fsend.at[other], frecv.at[other], (row, other)).wait_recv()

    begin_sum(0, fown[...])
    loads[3].wait()
    loads[4].wait()
    oself[...] = tn_dot(self_ref[...], fown[...])

    @pl.loop(1, NSLAB)
    def _(d):
        f_copy(wrap(slab + d, NSLAB)).wait_send()

    @pl.loop(0, NZ)
    def _(zz):
        @pl.when((z < NZ - 1) & (zz <= z))
        def _():
            z_copy(0, zz).wait_send()

        @pl.when((z > 0) & (zz >= z))
        def _():
            z_copy(1, zz).wait_send()

        for way in range(2):
            y_copy(way, zz).wait_send()
            h_copy(way, zz).wait_send()

        @pl.loop(0, NY)
        def _(yy):
            c_copy(yy, zz).wait_send()

    after_a(0)
    for peer in a_peers:
        a_copy(0, peer).wait_send()

    @pl.loop(1, NSLAB)
    def _(d):
        other = wrap(slab + d, NSLAB)
        dst = mown.at[pl.ds(pl.multiple_of(other * PART, PART), PART), :]
        remote(mean.at[other], dst, msend.at[other], mrecv.at[other], (row, other)).wait_recv()

    begin_sum(1, mown[...])
    after_a(1)
    for yy in y_peers:
        b_copy(yy).start()
    total = acc[y]
    for yy in y_peers:
        b_copy(yy, True).wait_recv()
        total = total + rb[yy]
    acc2[...] = total
    for hh in h_peers:
        hi_copy(hh).start()
    out_ref[...] = (oself[...] + tn_dot(neigh_ref[...], mown[...])).astype(jnp.bfloat16)
    for peer in a_peers:
        a_copy(1, peer).wait_send()
    for yy in y_peers:
        b_copy(yy).wait_send()

    @pl.loop(1, NSLAB)
    def _(d):
        m_copy(wrap(slab + d, NSLAB)).wait_send()

    total = acc2[hi]
    for hh in h_peers:
        hi_copy(hh, True).wait_recv()
        total = total + rh[hh]
    rz[z] = total
    for zz in z_peers:
        zl_copy(zz).start()
    for hh in h_peers:
        hi_copy(hh).wait_send()
    for zz in z_peers:
        zl_copy(zz, True).wait_recv()
    total = rz[0]
    for i in range(1, NZ):
        total = total + rz[i]
    rd[y, core] = total * factor
    for peer in d_peers:
        d_copy(peer).start()
    for zz in z_peers:
        zl_copy(zz).wait_send()
    for peer in d_peers:
        d_copy(peer, True).wait_recv()
    for q, ref in enumerate((gself_ref, gneigh_ref)):
        for e in range(2):
            for c in range(NC):
                ref[e * 8 : (e + 1) * 8, c * TILE : (c + 1) * TILE] = rd[2 * q + e, c]
    for peer in d_peers:
        d_copy(peer).wait_send()


def per_device(
    features, self_weight, neigh_weight, cotangent, degree, tile_count, tile_cols, tile_vals
):
    width, nodes = features.shape
    tiles, slots = tile_cols.shape
    factor = 1.0 / math.sqrt(nodes * NROW)
    owner = tile_cols // tiles
    place = (owner % NC * (NROW // NC) + owner // NC) * tiles + tile_cols % tiles
    used = jnp.arange(slots)[None, :] < tile_count[:, None]
    index = jnp.where(used, place, NROW * tiles).T
    f32, bf16 = jnp.float32, jnp.bfloat16
    vmem = pltpu.VMEM
    dma = pltpu.SemaphoreType.DMA
    in_vmem = pl.BlockSpec(memory_space=pltpu.VMEM)
    return pl.pallas_call(
        functools.partial(kernel, factor),
        out_shape=(
            jax.ShapeDtypeStruct((WIDTH, WIDTH), bf16),
            jax.ShapeDtypeStruct((width, WIDTH), f32),
            jax.ShapeDtypeStruct((width, WIDTH), f32),
        ),
        in_specs=[pl.BlockSpec(memory_space=pltpu.SMEM)] + [pl.BlockSpec(memory_space=pl.ANY)] * 6,
        out_specs=(in_vmem, in_vmem, in_vmem),
        scratch_shapes=[
            vmem((width, nodes), bf16),
            vmem(tile_vals.shape, bf16),
            vmem((WIDTH, WIDTH), bf16),
            vmem((WIDTH, WIDTH), bf16),
            vmem((tiles, TILE), jnp.int32),
            vmem((NROW * tiles + 1, width, TILE), bf16),
            vmem((WIDTH, WIDTH), bf16),
            vmem((WIDTH, WIDTH), bf16),
            vmem((NSLAB, width, WIDTH), bf16),
            vmem((WIDTH, WIDTH), bf16),
            vmem((WIDTH, WIDTH), f32),
            vmem((2, NC, NX, 2, NH, 8, TILE), f32),
            vmem((2, NC, NX, 2, NH, 8, TILE), f32),
            vmem((NY, NH, 8, TILE), f32),
            vmem((NY, NH, 8, TILE), f32),
            vmem((NH, 8, TILE), f32),
            vmem((NH, 8, TILE), f32),
            vmem((NZ, 8, TILE), f32),
            vmem((NY, NC, 8, TILE), f32),
            pltpu.SemaphoreType.REGULAR((len(ROUNDS), 2)),
            dma((6,)),
            dma((2, NZ)),
            dma((2, NZ)),
            dma((2, NZ)),
            dma((NY, NZ)),
            dma((NY, NZ)),
            dma((2, NZ)),
            dma((NY, NZ)),
            dma((NSLAB,)),
            dma((NSLAB,)),
            dma((NSLAB,)),
            dma((NSLAB,)),
            dma((2, NC, NX)),
            dma((2, NC, NX)),
            dma((NY,)),
            dma((NY,)),
            dma((NH,)),
            dma((NH,)),
            dma((NZ,)),
            dma((NZ,)),
            dma((NY, NC)),
            dma((NY, NC)),
        ],
        compiler_params=pltpu.CompilerParams(
            collective_id=0, has_side_effects=True, vmem_limit_bytes=60 * 1024 * 1024
        ),
    )(
        index,
        features,
        tile_vals,
        cotangent,
        self_weight,
        neigh_weight,
        degree.reshape(tiles, TILE),
    )


def solution(mesh):
    return jax.shard_map(
        per_device,
        mesh=mesh,
        in_specs=(
            P("slab", "row"),
            P(),
            P(),
            P(None, ("row", "slab")),
            P("row"),
            P("row"),
            P("row", None),
            P("row", None, None, None),
        ),
        out_specs=(P(None, ("row", "slab")), P("slab", None), P("slab", None)),
        check_vma=False,
    )
```
